32 devices in a mesh: row: 8 (over z, x), col: 4 (over y, core).
Axes of the slice: x: 2, y: 2, z: 4, core: 2. Of those that a mesh axis runs over, the one named last changes fastest.
Arguments:
- iterate: float32 [3584, 9216], P('row', 'col'), may hold values from -0.09375 to 0.09375
Outputs:
- update: float32 [3584, 9216], P('row', 'col')
The draws below stay inside these ranges and needn't reach their ends.
All inputs are finite; a program needn't handle non-finite values.
Results may differ from the reference program's by a relative error of at most 0.000068.
Values sent between devices are 32-bit elements; how exact they have to be, the bound alone decides.
A program may use at most 128 MiB of HBM per device.

```python
import math
import jax
import jax.numpy as jnp
from jax import lax

M = 3584
N = 9216


def draw_iterate(key, part):
    key = jax.random.fold_in(key, 11)
    key_noise, key_rows, key_cols = jax.random.split(key, 3)
    noise = jax.random.truncated_normal(key_noise, -6.0, 6.0, (M, N), jnp.float32)
    row_scale = jnp.exp(jax.random.uniform(key_rows, (M, 1), jnp.float32) * math.log(10.0))
    col_scale = jnp.exp(jax.random.uniform(key_cols, (1, N), jnp.float32) * math.log(10.0))
    factor = 0.3 / (21.0 * math.sqrt(N))
    return noise * row_scale * col_scale * factor


def setup_inputs(seed: int = 0) -> dict:
    splits = jax.random.split(jax.random.key(seed), 2)
    iterate = draw_iterate(jax.random.fold_in(splits[1], 71), 0)
    return {"iterate": iterate}


HIGHEST_PREC = lax.Precision.HIGHEST
COEF_A = 3.4445
COEF_B = -4.775
COEF_C = 2.0315

def reference(iterate):
    gram = jnp.dot(iterate, iterate.T, precision=HIGHEST_PREC, preferred_element_type=jnp.float32)
    gram_sq = jnp.dot(gram, gram, precision=HIGHEST_PREC, preferred_element_type=jnp.float32)
    poly = COEF_B * gram + COEF_C * gram_sq
    applied = jnp.dot(poly, iterate, precision=HIGHEST_PREC, preferred_element_type=jnp.float32)
    return (COEF_A * iterate + applied) * (0.2 * math.sqrt(max(M, N)))
```

```python
import math

import jax
import jax.numpy as jnp
from jax import lax
from jax.sharding import PartitionSpec as P

PREC = lax.Precision.HIGH
COEF_A = 3.4445
COEF_B = -4.775
COEF_C = 2.0315
CHUNKS = 3


def matmul(left, right):
    return jnp.dot(left, right, precision=PREC, preferred_element_type=jnp.float32)


def body(scale, iterate):
    col_count = lax.axis_size("col")
    width = iterate.shape[1] // CHUNKS
    pieces = [iterate[:, k * width : (k + 1) * width] for k in range(CHUNKS)]
    slabs = [lax.all_gather(piece, "row", axis=0, tiled=True) for piece in pieces]
    partial_value = None
    for piece, slab in zip(pieces, slabs):
        term = matmul(piece, slab.T)
        partial_value = term if partial_value is None else partial_value + term
    gram_panel = lax.psum(partial_value, "col")
    tile_width = gram_panel.shape[1] // col_count
    my_col = lax.axis_index("col")
    gram_tile = lax.dynamic_slice_in_dim(gram_panel, my_col * tile_width, tile_width, 1)
    gram_column = lax.all_gather(gram_tile, "row", axis=0, tiled=True)
    square_tile = matmul(gram_panel, gram_column)
    poly_tile = COEF_B * gram_tile + COEF_C * square_tile
    poly_panel = lax.all_gather(poly_tile, "col", axis=1, tiled=True)
    outs = [
        (COEF_A * piece + matmul(poly_panel, slab)) * scale
        for piece, slab in zip(pieces, slabs)
    ]
    return jnp.concatenate(outs, axis=1)


def solution(mesh):
    placed = P("row", "col")

    def run(iterate):
        scale = 0.2 * math.sqrt(max(iterate.shape))
        return jax.shard_map(
            lambda block: body(scale, block),
            mesh=mesh,
            in_specs=(placed,),
            out_specs=placed,
            check_vma=False,
        )(iterate)

    return run
```

```python
import math

import jax
import jax.numpy as jnp
from jax import lax
from jax.sharding import PartitionSpec as P

PREC = lax.Precision.HIGH
COEF_A = 3.4445
COEF_B = -4.775
COEF_C = 2.0315


def product(left, right, dims):
    return lax.dot_general(
        left, right, (dims, ((), ())), precision=PREC, preferred_element_type=jnp.float32
    )


def ring_order(count):
    return list(range(0, count, 2)) + list(range(1, count, 2))[::-1]


def shift(value, order, step):
    count = len(order)
    pairs = [(order[k], order[(k + step) % count]) for k in range(count)]
    return lax.ppermute(value, "row", pairs)


def swap(value, bit):
    count = lax.axis_size("col")
    return lax.ppermute(value, "col", [(k, k ^ bit) for k in range(count)])


def ring_gather(up, down, order, visit):
    count = len(order)
    table = jnp.array(order, jnp.int32)
    place = jnp.array([order.index(k) for k in range(count)], jnp.int32)
    me = lax.axis_index("row")
    mine = place[me]
    visit(0, up, me)
    visit(1, down, me)
    for step in range(1, count):
        up = shift(up, order, 1)
        down = shift(down, order, -1)
        visit(0, up, table[(mine - step) % count])
        visit(1, down, table[(mine + step) % count])


def body(scale, iterate):
    rows, cols = iterate.shape
    row_count, col_count = lax.axis_size("row"), lax.axis_size("col")
    total = rows * row_count
    order = ring_order(row_count)
    me, my_col = lax.axis_index("row"), lax.axis_index("col")
    half = cols // 2
    own = [iterate[:, :half], iterate[:, half:]]

    slabs = [jnp.zeros((total, half), jnp.float32) for _ in range(2)]
    panels = [jnp.zeros((total, rows), jnp.float32) for _ in range(2)]

    def take_rows(which, value, owner):
        slabs[which] = lax.dynamic_update_slice(slabs[which], value, (owner * rows, 0))
        block = product(value, own[which], ((1,), (1,)))
        panels[which] = lax.dynamic_update_slice(panels[which], block, (owner * rows, 0))

    ring_gather(own[0], own[1], order, take_rows)
    partial_value = panels[0] + panels[1]

    tile = partial_value
    bit = 1
    while bit < col_count:
        size = tile.shape[0] // 2
        upper = (my_col & bit) != 0
        low, high = tile[:size], tile[size:]
        tile = jnp.where(upper, high, low) + swap(jnp.where(upper, low, high), bit)
        bit *= 2

    def double(value, axis):
        bit = col_count // 2
        while bit:
            other = swap(value, bit)
            upper = (my_col & bit) != 0
            value = jnp.concatenate(
                [jnp.where(upper, other, value), jnp.where(upper, value, other)], axis
            )
            bit //= 2
        return value

    gram_tile = tile.T
    width = gram_tile.shape[1]
    column = [jnp.zeros((total, width), jnp.float32)]
    near = rows // 16 * 8

    def take_tile(which, value, owner):
        column[0] = lax.dynamic_update_slice(
            column[0], value, (owner * rows + (near if which else 0), 0)
        )

    ring_gather(gram_tile[:near], gram_tile[near:], order, take_tile)
    panel = double(tile, 0)
    square_tile = product(panel, column[0], ((0,), (0,)))
    poly_panel = double(COEF_B * gram_tile + COEF_C * square_tile, 1)
    outs = [
        (COEF_A * piece + product(poly_panel, slab, ((1,), (0,)))) * scale
        for piece, slab in zip(own, slabs)
    ]
    return jnp.concatenate(outs, axis=1)


def solution(mesh):
    placed = P("row", "col")

    def run(iterate):
        scale = 0.2 * math.sqrt(max(iterate.shape))
        return jax.shard_map(
            lambda block: body(scale, block),
            mesh=mesh,
            in_specs=(placed,),
            out_specs=placed,
            check_vma=False,
        )(iterate)

    return run
```

```python
import math

import jax
import jax.numpy as jnp
from jax import lax
from jax.sharding import PartitionSpec as P

PREC = lax.Precision.HIGH
COEF_A = 3.4445
COEF_B = -4.775
COEF_C = 2.0315


def product(left, right, dims):
    return lax.dot_general(
        left, right, (dims, ((), ())), precision=PREC, preferred_element_type=jnp.float32
    )


def ring_order(count):
    return list(range(0, count, 2)) + list(range(1, count, 2))[::-1]


def shift(value, order, step):
    count = len(order)
    pairs = [(order[k], order[(k + step) % count]) for k in range(count)]
    return lax.ppermute(value, "row", pairs)


def swap(value, bit):
    count = lax.axis_size("col")
    return lax.ppermute(value, "col", [(k, k ^ bit) for k in range(count)])


def sum_over_col(low, high, upper):
    mine = jnp.where(upper, high, low) + swap(jnp.where(upper, low, high), 1)
    bit = 2
    while bit < lax.axis_size("col"):
        mine = mine + swap(mine, bit)
        bit *= 2
    other = swap(mine, 1)
    return jnp.where(upper, other, mine), jnp.where(upper, mine, other)


def body(scale, iterate):
    rows, cols = iterate.shape
    row_count, col_count = lax.axis_size("row"), lax.axis_size("col")
    total = rows * row_count
    near = rows // 2
    per = row_count // col_count
    width = per * rows
    order = ring_order(row_count)
    place = jnp.array([order.index(k) for k in range(row_count)], jnp.int32)
    mine = place[lax.axis_index("row")]
    my_col = lax.axis_index("col")
    upper = (my_col & 1) != 0

    up, down = iterate[:near], iterate[near:]
    near_blocks, far_blocks = [], []
    slab = None
    for step in range(row_count):
        last = step == row_count - 1
        if not last:
            next_up, next_down = shift(up, order, 1), shift(down, order, -1)
        near_at = (mine - step) % row_count * rows
        far_at = (mine + step) % row_count * rows + near
        if step == 1:
            slab = jnp.broadcast_to(up[:1], (total, cols))
            own_at = mine * rows
            slab = lax.dynamic_update_slice(slab, iterate, (own_at, 0))
        if step >= 1:
            slab = lax.dynamic_update_slice(slab, up, (near_at, 0))
            slab = lax.dynamic_update_slice(slab, down, (far_at, 0))
        near_part = product(up, iterate, ((1,), (1,)))
        far_part = product(down, iterate, ((1,), (1,)))
        near_part, far_part = sum_over_col(near_part, far_part, upper)
        if not last:
            held = (next_up, next_down, near_part, far_part)
            if slab is None:
                next_up, next_down, near_part, far_part = lax.optimization_barrier(held)
            else:
                next_up, next_down, near_part, far_part, slab = lax.optimization_barrier(
                    held + (slab,)
                )
            up, down = next_up, next_down
        near_blocks.append(near_part)
        far_blocks.append(far_part)

    near_all = jnp.stack(near_blocks)
    far_all = jnp.stack(far_blocks)
    parts = []
    for k in range(per):
        at = my_col * per + k
        parts.append(lax.dynamic_index_in_dim(near_all, (mine - at) % row_count, 0, False))
        parts.append(lax.dynamic_index_in_dim(far_all, (at - mine) % row_count, 0, False))
    gram_tile = jnp.concatenate(parts, axis=0).T

    up, down = gram_tile[:near], gram_tile[near:]
    square_tile = None
    for step in range(row_count):
        last = step == row_count - 1
        if not last:
            next_up, next_down = shift(up, order, 1), shift(down, order, -1)
        term = product(near_blocks[step], up, ((0,), (0,)))
        term = term + product(far_blocks[step], down, ((0,), (0,)))
        square_tile = term if square_tile is None else square_tile + term
        if not last:
            up, down, square_tile = lax.optimization_barrier((next_up, next_down, square_tile))
    poly_tile = COEF_B * gram_tile + COEF_C * square_tile

    tiles = {0: poly_tile}
    for k in range(1, col_count):
        low_bit = k & -k
        tiles[k] = swap(tiles[k ^ low_bit], low_bit)
    applied = None
    for k in range(0, col_count, 2):
        pair = jnp.concatenate(
            [
                jnp.where(upper, tiles[k + 1], tiles[k]),
                jnp.where(upper, tiles[k], tiles[k + 1]),
            ],
            axis=1,
        )
        at = ((my_col ^ k) >> 1) * (2 * width)
        term = product(pair, lax.dynamic_slice_in_dim(slab, at, 2 * width, 0), ((1,), (0,)))
        applied = term if applied is None else applied + term
    return (COEF_A * iterate + applied) * scale


def solution(mesh):
    placed = P("row", "col")

    def run(iterate):
        scale = 0.2 * math.sqrt(max(iterate.shape))
        return jax.shard_map(
            lambda block: body(scale, block),
            mesh=mesh,
            in_specs=(placed,),
            out_specs=placed,
            check_vma=False,
        )(iterate)

    return run
```

```python
import math

import jax
import jax.numpy as jnp
from jax import lax
from jax.sharding import PartitionSpec as P

PREC = lax.Precision.HIGH
COEF_A = 3.4445
COEF_B = -4.775
COEF_C = 2.0315


def product(left, right, dims):
    return lax.dot_general(
        left, right, (dims, ((), ())), precision=PREC, preferred_element_type=jnp.float32
    )


def ring_order(count):
    return list(range(0, count, 2)) + list(range(1, count, 2))[::-1]


def shift(value, order, step):
    count = len(order)
    pairs = [(order[k], order[(k + step) % count]) for k in range(count)]
    return lax.ppermute(value, "row", pairs)


def swap(value, bit):
    count = lax.axis_size("col")
    return lax.ppermute(value, "col", [(k, k ^ bit) for k in range(count)])


def sum_over_col(low, high, upper):
    mine = jnp.where(upper, high, low) + swap(jnp.where(upper, low, high), 1)
    bit = 2
    while bit < lax.axis_size("col"):
        mine = mine + swap(mine, bit)
        bit *= 2
    other = swap(mine, 1)
    return jnp.where(upper, other, mine), jnp.where(upper, mine, other)


def body(scale, iterate):
    rows, cols = iterate.shape
    row_count, col_count = lax.axis_size("row"), lax.axis_size("col")
    total = rows * row_count
    near = rows // 2
    per = row_count // col_count
    width = per * rows
    order = ring_order(row_count)
    place = jnp.array([order.index(k) for k in range(row_count)], jnp.int32)
    mine = place[lax.axis_index("row")]
    my_col = lax.axis_index("col")
    upper = (my_col & 1) != 0

    up, down = iterate[:near], iterate[near:]
    near_blocks, far_blocks = [], []
    slab = None
    for step in range(row_count):
        last = step == row_count - 1
        if not last:
            next_up, next_down = shift(up, order, 1), shift(down, order, -1)
        near_at = (mine - step) % row_count * rows
        far_at = (mine + step) % row_count * rows + near
        if step == 1:
            slab = jnp.broadcast_to(up[:1], (total, cols))
            own_at = mine * rows
            slab = lax.dynamic_update_slice(slab, iterate, (own_at, 0))
        if step >= 1:
            slab = lax.dynamic_update_slice(slab, up, (near_at, 0))
            slab = lax.dynamic_update_slice(slab, down, (far_at, 0))
        near_part = product(up, iterate, ((1,), (1,)))
        far_part = product(down, iterate, ((1,), (1,)))
        waiting = [near_part, far_part]
        if step >= row_count - 2:
            waiting = list(sum_over_col(near_part, far_part, upper))
        if not last:
            held = [next_up, next_down] + waiting
            if step >= 1:
                held += [slab]
                if step < row_count - 2:
                    held += [near_blocks.pop(), far_blocks.pop()]
            held = list(lax.optimization_barrier(tuple(held)))
            up, down, near_part, far_part = held[:4]
            waiting = held[2:4]
            if step >= 1:
                slab = held[4]
                if step < row_count - 2:
                    near_blocks.append(held[5])
                    far_blocks.append(held[6])
            if step < row_count - 2:
                waiting = sum_over_col(near_part, far_part, upper)
        near_blocks.append(waiting[0])
        far_blocks.append(waiting[1])

    near_all = jnp.concatenate(near_blocks, axis=0)
    far_all = jnp.concatenate(far_blocks, axis=0)
    parts = []
    for k in range(per):
        at = my_col * per + k
        parts.append(lax.dynamic_slice_in_dim(near_all, (mine - at) % row_count * near, near))
        parts.append(lax.dynamic_slice_in_dim(far_all, (at - mine) % row_count * near, near))
    gram_tile = jnp.concatenate(parts, axis=0).T

    up, down = gram_tile[:near], gram_tile[near:]
    square_tile = None
    for step in range(row_count):
        last = step == row_count - 1
        if not last:
            next_up, next_down = shift(up, order, 1), shift(down, order, -1)
        term = product(near_blocks[step], up, ((0,), (0,)))
        term = term + product(far_blocks[step], down, ((0,), (0,)))
        square_tile = term if square_tile is None else square_tile + term
        if not last:
            up, down, square_tile = lax.optimization_barrier((next_up, next_down, square_tile))
    poly_tile = COEF_B * gram_tile + COEF_C * square_tile

    tiles = {0: poly_tile}
    for k in range(1, col_count):
        low_bit = k & -k
        if low_bit == 1 and k > 1:
            continue
        tiles[k] = swap(tiles[k ^ low_bit], low_bit)
    applied = None
    for k in range(0, col_count, 2):
        if applied is not None:
            tiles[k], applied = lax.optimization_barrier((tiles[k], applied))
            tiles[k + 1] = swap(tiles[k], 1)
        pair = jnp.concatenate(
            [
                jnp.where(upper, tiles[k + 1], tiles[k]),
                jnp.where(upper, tiles[k], tiles[k + 1]),
            ],
            axis=1,
        )
        at = ((my_col ^ k) >> 1) * (2 * width)
        term = product(pair, lax.dynamic_slice_in_dim(slab, at, 2 * width, 0), ((1,), (0,)))
        applied = term if applied is None else applied + term
    return (COEF_A * iterate + applied) * scale


def solution(mesh):
    placed = P("row", "col")

    def run(iterate):
        scale = 0.2 * math.sqrt(max(iterate.shape))
        return jax.shard_map(
            lambda block: body(scale, block),
            mesh=mesh,
            in_specs=(placed,),
            out_specs=placed,
            check_vma=False,
        )(iterate)

    return run
```

```python
import math

import jax
import jax.numpy as jnp
from jax import lax
from jax.sharding import PartitionSpec as P

PREC = lax.Precision.HIGH
COEF_A = 3.4445
COEF_B = -4.775
COEF_C = 2.0315


def product(left, right, dims):
    return lax.dot_general(
        left, right, (dims, ((), ())), precision=PREC, preferred_element_type=jnp.float32
    )


def split(value):
    high = lax.reduce_precision(value, exponent_bits=8, mantissa_bits=7)
    return high.astype(jnp.bfloat16), (value - high).astype(jnp.bfloat16)


def keep(slab, value, at, span):
    high, low = split(value)
    to = at // span * (2 * span) + at % span
    slab = lax.dynamic_update_slice(slab, high, (to, 0))
    return lax.dynamic_update_slice(slab, low, (to + span, 0))


def ring_order(count):
    return list(range(0, count, 2)) + list(range(1, count, 2))[::-1]


def shift(value, order, step):
    count = len(order)
    pairs = [(order[k], order[(k + step) % count]) for k in range(count)]
    return lax.ppermute(value, "row", pairs)


def swap(value, bit):
    count = lax.axis_size("col")
    return lax.ppermute(value, "col", [(k, k ^ bit) for k in range(count)])


def core_sum(low, high, upper):
    return jnp.where(upper, high, low) + swap(jnp.where(upper, low, high), 1)


def chip_sum(mine, upper):
    bit = 2
    while bit < lax.axis_size("col"):
        mine = mine + swap(mine, bit)
        bit *= 2
    other = swap(mine, 1)
    return jnp.where(upper, other, mine), jnp.where(upper, mine, other)


def body(scale, iterate):
    rows, cols = iterate.shape
    row_count, col_count = lax.axis_size("row"), lax.axis_size("col")
    total = rows * row_count
    near = rows // 2
    per = row_count // col_count
    width = per * rows
    order = ring_order(row_count)
    place = jnp.array([order.index(k) for k in range(row_count)], jnp.int32)
    mine = place[lax.axis_index("row")]
    my_col = lax.axis_index("col")
    upper = (my_col & 1) != 0

    up, down = iterate[:near], iterate[near:]
    blocks = []
    half_summed = raw = None
    slab = None
    for step in range(row_count):
        last = step == row_count - 1
        if not last:
            next_up, next_down = shift(up, order, 1), shift(down, order, -1)
        near_at = (mine - step) % row_count * rows
        far_at = (mine + step) % row_count * rows + near
        if step == 1:
            slab = jnp.broadcast_to(up[:1].astype(jnp.bfloat16), (2 * total, cols))
            slab = keep(slab, iterate, mine * rows, 2 * width)
        if step >= 1:
            slab = keep(slab, up, near_at, 2 * width)
            slab = keep(slab, down, far_at, 2 * width)
        near_part = product(up, iterate, ((1,), (1,)))
        far_part = product(down, iterate, ((1,), (1,)))
        finished = []
        if step < row_count - 2:
            if half_summed is not None:
                finished.append(chip_sum(half_summed, upper))
            half_summed = None if raw is None else core_sum(*raw, upper)
            raw = (near_part, far_part)
        else:
            if half_summed is not None:
                finished.append(chip_sum(half_summed, upper))
            if raw is not None:
                finished.append(chip_sum(core_sum(*raw, upper), upper))
            half_summed, raw = core_sum(near_part, far_part, upper), None
            if last:
                finished.append(chip_sum(half_summed, upper))
        if not last:
            held = ((next_up, next_down), finished, half_summed, raw, slab)
            (up, down), finished, half_summed, raw, slab = lax.optimization_barrier(held)
        blocks += finished

    near_blocks, far_blocks = zip(*blocks)
    near_all = jnp.concatenate(near_blocks, axis=0)
    far_all = jnp.concatenate(far_blocks, axis=0)
    parts = []
    for k in range(per):
        at = my_col * per + k
        parts.append(lax.dynamic_slice_in_dim(near_all, (mine - at) % row_count * near, near))
        parts.append(lax.dynamic_slice_in_dim(far_all, (at - mine) % row_count * near, near))
    gram_tile = jnp.concatenate(parts, axis=0).T

    up, down = gram_tile[:near], gram_tile[near:]
    square_tile = None
    for step in range(row_count):
        last = step == row_count - 1
        if not last:
            next_up, next_down = shift(up, order, 1), shift(down, order, -1)
        term = product(near_blocks[step], up, ((0,), (0,)))
        term = term + product(far_blocks[step], down, ((0,), (0,)))
        square_tile = term if square_tile is None else square_tile + term
        if not last:
            up, down, square_tile, slab = lax.optimization_barrier(
                (next_up, next_down, square_tile, slab)
            )
    poly_tile = COEF_B * gram_tile + COEF_C * square_tile

    tiles = {0: poly_tile}
    for k in range(1, col_count):
        low_bit = k & -k
        if low_bit == 1 and k > 1:
            continue
        tiles[k] = swap(tiles[k ^ low_bit], low_bit)
    applied = None
    for k in range(0, col_count, 2):
        if applied is not None:
            tiles[k], applied = lax.optimization_barrier((tiles[k], applied))
            tiles[k + 1] = swap(tiles[k], 1)
        pair = jnp.concatenate(
            [
                jnp.where(upper, tiles[k + 1], tiles[k]),
                jnp.where(upper, tiles[k], tiles[k + 1]),
            ],
            axis=1,
        )
        high, low = split(pair)
        at = ((my_col ^ k) >> 1) * (4 * width)
        kept = lax.dynamic_slice_in_dim(slab, at, 4 * width, 0)
        term = jnp.dot(
            jnp.concatenate([high, high], axis=1), kept, preferred_element_type=jnp.float32
        )
        term = term + jnp.dot(low, kept[: 2 * width], preferred_element_type=jnp.float32)
        applied = term if applied is None else applied + term
    return (COEF_A * iterate + applied) * scale


def solution(mesh):
    placed = P("row", "col")

    def run(iterate):
        scale = 0.2 * math.sqrt(max(iterate.shape))
        return jax.shard_map(
            lambda block: body(scale, block),
            mesh=mesh,
            in_specs=(placed,),
            out_specs=placed,
            check_vma=False,
        )(iterate)

    return run
```

```python
import math

import jax
import jax.numpy as jnp
from jax import lax
from jax.sharding import PartitionSpec as P

PREC = lax.Precision.HIGH
COEF_A = 3.4445
COEF_B = -4.775
COEF_C = 2.0315


def product(left, right, dims):
    return lax.dot_general(
        left, right, (dims, ((), ())), precision=PREC, preferred_element_type=jnp.float32
    )


def ring_order(count):
    return list(range(0, count, 2)) + list(range(1, count, 2))[::-1]


def shift(value, order, step):
    count = len(order)
    pairs = [(order[k], order[(k + step) % count]) for k in range(count)]
    return lax.ppermute(value, "row", pairs)


def swap(value, bit):
    count = lax.axis_size("col")
    return lax.ppermute(value, "col", [(k, k ^ bit) for k in range(count)])


def sum_over_col(low, high, upper):
    mine = jnp.where(upper, high, low) + swap(jnp.where(upper, low, high), 1)
    bit = 2
    while bit < lax.axis_size("col"):
        mine = mine + swap(mine, bit)
        bit *= 2
    other = swap(mine, 1)
    return jnp.where(upper, other, mine), jnp.where(upper, mine, other)


def body(scale, iterate):
    rows, cols = iterate.shape
    row_count, col_count = lax.axis_size("row"), lax.axis_size("col")
    total = rows * row_count
    near = rows // 2
    per = row_count // col_count
    width = per * rows
    order = ring_order(row_count)
    place = jnp.array([order.index(k) for k in range(row_count)], jnp.int32)
    mine = place[lax.axis_index("row")]
    my_col = lax.axis_index("col")
    upper = (my_col & 1) != 0

    up, down = iterate[:near], iterate[near:]
    near_blocks, far_blocks = [], []
    slab = None
    for step in range(row_count):
        last = step == row_count - 1
        if not last:
            next_up, next_down = shift(up, order, 1), shift(down, order, -1)
        near_at = (mine - step) % row_count * rows
        far_at = (mine + step) % row_count * rows + near
        if step == 1:
            slab = jnp.broadcast_to(up[:1], (total, cols))
            own_at = mine * rows
            slab = lax.dynamic_update_slice(slab, iterate, (own_at, 0))
        if step >= 1:
            slab = lax.dynamic_update_slice(slab, up, (near_at, 0))
            slab = lax.dynamic_update_slice(slab, down, (far_at, 0))
        near_part = product(up, iterate, ((1,), (1,)))
        far_part = product(down, iterate, ((1,), (1,)))
        near_part, far_part = sum_over_col(near_part, far_part, upper)
        if not last:
            held = (next_up, next_down, near_part, far_part)
            if slab is None:
                next_up, next_down, near_part, far_part = lax.optimization_barrier(held)
            else:
                next_up, next_down, near_part, far_part, slab = lax.optimization_barrier(
                    held + (slab,)
                )
            up, down = next_up, next_down
        near_blocks.append(near_part)
        far_blocks.append(far_part)

    near_all = jnp.concatenate(near_blocks, axis=0)
    far_all = jnp.concatenate(far_blocks, axis=0)
    parts = []
    for k in range(per):
        at = my_col * per + k
        parts.append(lax.dynamic_slice_in_dim(near_all, (mine - at) % row_count * near, near))
        parts.append(lax.dynamic_slice_in_dim(far_all, (at - mine) % row_count * near, near))
    gram_tile = jnp.concatenate(parts, axis=0).T

    up, down = gram_tile[:near], gram_tile[near:]
    square_tile = None
    for step in range(row_count):
        last = step == row_count - 1
        if not last:
            next_up, next_down = shift(up, order, 1), shift(down, order, -1)
        term = product(near_blocks[step], up, ((0,), (0,)))
        term = term + product(far_blocks[step], down, ((0,), (0,)))
        square_tile = term if square_tile is None else square_tile + term
        if not last:
            up, down, square_tile, slab = lax.optimization_barrier(
                (next_up, next_down, square_tile, slab)
            )
    poly_tile = COEF_B * gram_tile + COEF_C * square_tile

    tiles = {0: poly_tile}
    for k in range(1, col_count):
        low_bit = k & -k
        if low_bit == 1 and k > 1:
            continue
        tiles[k] = swap(tiles[k ^ low_bit], low_bit)
    applied = None
    for k in range(0, col_count, 2):
        if applied is not None:
            tiles[k], applied = lax.optimization_barrier((tiles[k], applied))
            tiles[k + 1] = swap(tiles[k], 1)
        pair = jnp.concatenate(
            [
                jnp.where(upper, tiles[k + 1], tiles[k]),
                jnp.where(upper, tiles[k], tiles[k + 1]),
            ],
            axis=1,
        )
        at = ((my_col ^ k) >> 1) * (2 * width)
        term = product(pair, lax.dynamic_slice_in_dim(slab, at, 2 * width, 0), ((1,), (0,)))
        applied = term if applied is None else applied + term
    return (COEF_A * iterate + applied) * scale


def solution(mesh):
    placed = P("row", "col")

    def run(iterate):
        scale = 0.2 * math.sqrt(max(iterate.shape))
        return jax.shard_map(
            lambda block: body(scale, block),
            mesh=mesh,
            in_specs=(placed,),
            out_specs=placed,
            check_vma=False,
        )(iterate)

    return run
```
